128 devices in a mesh: grid: 16 (over x, z_lo, core), tm: 8 (over z_hi, y).
Axes of the slice: x: 4, y: 4, z: 4 (z_hi: 2, z_lo: 2; z = z_hi * 2 + z_lo), core: 2. Of those that a mesh axis runs over, the one named last changes fastest.
Arguments:
- anomalies: float32 [32768, 8192], P('grid', 'tm'), may hold values from -2000 to 2000
- lag_list: int32 [8], replicated, may hold values from 0 to 168, as said below
- pair_plan: int32 [16, 3, 8, 2], P('grid'), may hold values from 0 to 15, as said below
Outputs:
- correlation: float32 [16, 3, 8, 8, 128, 128], P('grid', None, None, 'tm')
The draws below stay inside these ranges and needn't reach their ends.
Inputs may be any that keep to these rules, and one draw needn't show every extreme that they name: `lag_list`: ascending and distinct; the first is 0 and the last 168. `pair_plan`: for each block and offset, the second sub-blocks of the 8 pairs are distinct.
All inputs are finite; a program needn't handle non-finite values.
Results may differ from the reference program's by a relative error of at most 0.0003.
Values may be sent and summed in bfloat16 or wider, within the bound.
No kernel may reach another device: no remote copies, remote signals or barrier semaphores. Data moves between devices by JAX's collectives and lax.ppermute only.
A program may use at most 192 MiB of HBM per device.

```python
import math
import jax
import jax.numpy as jnp
from jax import lax

P_DEV = 2048
TM_DEV = 1024
SUB = 128
LAGS = 8
LAGMAX = 168
STEPS = 3
PAIRS = 8
POINTS = 32768
HOURS = 8192
N_GRID = 16
N_TM = 8


def draw_anomalies(key, part):
    key = jax.random.fold_in(key, 11)
    subkeys = jax.random.split(key, 6)
    hours_axis = jnp.arange(HOURS, dtype=jnp.float32)[None, :]
    scales = jnp.exp(jax.random.uniform(subkeys[0], (POINTS, 1), minval=0.0, maxval=math.log(10.0)))
    envelope = 1.0 + 2.0 * hours_axis / HOURS
    noise_part = jnp.clip(jax.random.normal(subkeys[1], (POINTS, HOURS)), -4.0, 4.0)
    offsets = 0.5 * jnp.clip(jax.random.normal(subkeys[2], (POINTS, 1)), -3.0, 3.0)
    weights = jnp.clip(jax.random.normal(subkeys[3], (POINTS, 4)), -4.0, 4.0)
    phases = jax.random.uniform(subkeys[4], (POINTS, 4), minval=0.0, maxval=2.0 * math.pi)
    periods = jnp.exp(jax.random.uniform(subkeys[5], (4,), minval=math.log(24.0), maxval=math.log(720.0)))
    signal = 0.7 * noise_part + offsets
    for wave in range(4):
        signal = signal + weights[:, wave:wave + 1] * jnp.cos(2.0 * math.pi * hours_axis / periods[wave] + phases[:, wave:wave + 1])
    return (scales * envelope * signal).astype(jnp.float32)


def draw_lag_list(key, part):
    key = jax.random.fold_in(key, 23)
    shuffled = jax.random.permutation(key, LAGMAX - 1)[:LAGS - 2] + 1
    middle = jnp.sort(shuffled).astype(jnp.int32)
    return jnp.concatenate([jnp.zeros((1,), jnp.int32), middle, jnp.full((1,), LAGMAX, jnp.int32)])


def draw_pair_plan(key, part):
    key = jax.random.fold_in(key, 37)
    first_key, second_key = jax.random.split(key, 2)
    sub_count = P_DEV // SUB
    firsts = jax.random.randint(first_key, (N_GRID, STEPS, PAIRS), 0, sub_count).astype(jnp.int32)
    perm_keys = jax.random.split(second_key, N_GRID * STEPS)

    def one_perm(single_key):
        return jax.random.permutation(single_key, sub_count)[:PAIRS].astype(jnp.int32)
    seconds = jax.vmap(one_perm)(perm_keys).reshape(N_GRID, STEPS, PAIRS)
    return jnp.stack([firsts, seconds], axis=3).astype(jnp.int32)


def setup_inputs(seed: int = 0) -> dict:
    seeds = jax.random.split(jax.random.key(seed), 4)
    anomalies = draw_anomalies(jax.random.fold_in(seeds[3], 71), 0)
    lag_list = draw_lag_list(jax.random.fold_in(seeds[3], 71), 0)
    pair_plan = draw_pair_plan(jax.random.fold_in(seeds[3], 71), 0)
    return dict(anomalies=anomalies, lag_list=lag_list, pair_plan=pair_plan)


def reference(anomalies, lag_list, pair_plan):
    all_hours = anomalies.shape[1]
    totals = lax.optimization_barrier(jnp.sum(anomalies, axis=1))
    squares = lax.optimization_barrier(jnp.sum(anomalies * anomalies, axis=1))
    center = totals / all_hours
    spread = squares / all_hours - center * center
    scaled = ((anomalies - center[:, None]) * lax.rsqrt(spread + 1e-05)[:, None]).astype(jnp.bfloat16)
    padded = jnp.concatenate([scaled, jnp.zeros((scaled.shape[0], LAGMAX), jnp.bfloat16)], axis=1)
    blocks = scaled.reshape(N_GRID, P_DEV, all_hours)
    padded_blocks = padded.reshape(N_GRID, P_DEV, all_hours + LAGMAX)
    divisor = (all_hours - lag_list).astype(jnp.float32)

    def one_block(block_index):
        mine = lax.dynamic_index_in_dim(blocks, block_index, 0, keepdims=False)
        outputs = []
        for cycle_step in range(STEPS):
            other = ((block_index - cycle_step - 1) % N_GRID).astype(jnp.int32)
            partner = lax.dynamic_index_in_dim(padded_blocks, other, 0, keepdims=False)
            plan = lax.dynamic_index_in_dim(pair_plan, block_index, 0, keepdims=False)[cycle_step]

            def one_couple(couple):
                first_rows = lax.dynamic_slice_in_dim(mine, couple[0] * SUB, SUB, 0)
                second_rows = lax.dynamic_slice_in_dim(partner, couple[1] * SUB, SUB, 0)

                def take_offset(offset):
                    return lax.dynamic_slice_in_dim(second_rows, offset, all_hours, 1)
                shifted = jax.vmap(take_offset)(lag_list)
                first_wide = first_rows.astype(jnp.float32).reshape(SUB, N_TM, TM_DEV)
                second_wide = shifted.astype(jnp.float32).reshape(LAGS, SUB, N_TM, TM_DEV)
                pieces = jnp.einsum('cst,lbst->slcb', first_wide, second_wide)
                return lax.optimization_barrier(jnp.sum(pieces, axis=0))
            outputs.append(jax.vmap(one_couple)(plan) / divisor[None, :, None, None])
        return jnp.stack(outputs)
    return lax.map(one_block, jnp.arange(N_GRID, dtype=jnp.int32))
```

```python
import jax
import jax.numpy as jnp
from jax import lax
from jax.experimental import pallas as pl
from jax.experimental.pallas import tpu as pltpu
from jax.sharding import PartitionSpec as P

SUB = 128
LANES = 128
HALO = 256
STEPS = 3
RING = 4
CHUNKS = (
    (1, 0, 4, 0),
    (1, 4, 4, 1),
    (3, 0, 4, 0),
    (3, 4, 4, 1),
    (2, 0, 4, 0),
    (2, 4, 4, 1),
)
IN_FLIGHT = 2


def sums_kernel(x_ref, out_ref):
    for sub in range(4):
        rows = slice(sub * SUB, (sub + 1) * SUB)
        total = jnp.zeros((SUB, LANES), jnp.float32)
        square = jnp.zeros((SUB, LANES), jnp.float32)
        for tile in range(x_ref.shape[1] // LANES):
            value = x_ref[rows, tile * LANES:(tile + 1) * LANES]
            total = total + value
            square = square + value * value
        out_ref[sub:sub + 1, :] = jnp.sum(total.T, axis=0, keepdims=True)
        out_ref[4 + sub:5 + sub, :] = jnp.sum(square.T, axis=0, keepdims=True)


def local_sums(anomalies):
    points, hours = anomalies.shape
    steps = points // (4 * SUB)
    return pl.pallas_call(
        sums_kernel,
        grid=(steps,),
        in_specs=[pl.BlockSpec((4 * SUB, hours), lambda i: (i, 0))],
        out_specs=pl.BlockSpec((8, LANES), lambda i: (i, 0)),
        out_shape=jax.ShapeDtypeStruct((8 * steps, LANES), jnp.float32),
        compiler_params=pltpu.CompilerParams(vmem_limit_bytes=24 << 20),
        cost_estimate=pl.CostEstimate(
            flops=3 * points * hours, bytes_accessed=4 * points * hours, transcendentals=0
        ),
        name="local_sums",
    )(anomalies)


def scale_rows(x, center_row, inverse_row, store):
    center = jnp.broadcast_to(center_row, (SUB, LANES)).T
    inverse = jnp.broadcast_to(inverse_row, (SUB, LANES)).T
    for tile in range(x.shape[1] // LANES):
        cols = slice(tile * LANES, (tile + 1) * LANES)
        store(cols, ((x[:, cols] - center) * inverse).astype(jnp.bfloat16))


def pick_kernel(index_ref, x_ref, norm_ref, dep_ref, out_ref):
    sub = index_ref[pl.program_id(0)]

    def store(cols, value):
        out_ref[0, :, cols] = value

    scale_rows(x_ref.at[0], norm_ref[0, pl.ds(sub, 1), :], norm_ref[1, pl.ds(sub, 1), :], store)


def scaled_pick(index, blocks, norm, dep):
    count, hours = index.shape[0], blocks.shape[2]
    return pl.pallas_call(
        pick_kernel,
        grid_spec=pltpu.PrefetchScalarGridSpec(
            num_scalar_prefetch=1,
            grid=(count,),
            in_specs=[
                pl.BlockSpec((1, SUB, hours), lambda i, index: (index[i], 0, 0)),
                pl.BlockSpec(norm.shape, lambda i, index: (0, 0, 0)),
                pl.BlockSpec(memory_space=pl.ANY),
            ],
            out_specs=pl.BlockSpec((1, SUB, hours), lambda i, index: (i, 0, 0)),
        ),
        out_shape=jax.ShapeDtypeStruct((count, SUB, hours), jnp.bfloat16),
        compiler_params=pltpu.CompilerParams(vmem_limit_bytes=24 << 20),
        cost_estimate=pl.CostEstimate(
            flops=2 * count * SUB * hours, bytes_accessed=6 * count * SUB * hours, transcendentals=0
        ),
        name="scaled_pick",
    )(index, blocks, norm, dep)


def all_kernel(x_ref, norm_ref, dep_ref, out_ref, tail_ref):
    sub = pl.program_id(0)
    hours = x_ref.shape[2]

    def store(cols, value):
        out_ref[0, :, cols] = value
        if cols.start >= hours - HALO:
            tail_ref[0, :, cols.start - hours + HALO:cols.stop - hours + HALO] = value

    scale_rows(x_ref.at[0], norm_ref[0, pl.ds(sub, 1), :], norm_ref[1, pl.ds(sub, 1), :], store)


def scaled_all(blocks, norm, dep):
    count, _, hours = blocks.shape
    return pl.pallas_call(
        all_kernel,
        grid=(count,),
        in_specs=[
            pl.BlockSpec((1, SUB, hours), lambda i: (i, 0, 0)),
            pl.BlockSpec(norm.shape, lambda i: (0, 0, 0)),
            pl.BlockSpec(memory_space=pl.ANY),
        ],
        out_specs=[
            pl.BlockSpec((1, SUB, hours), lambda i: (i, 0, 0)),
            pl.BlockSpec((1, SUB, HALO), lambda i: (i, 0, 0)),
        ],
        out_shape=[
            jax.ShapeDtypeStruct((count, SUB, hours), jnp.bfloat16),
            jax.ShapeDtypeStruct((count, SUB, HALO), jnp.bfloat16),
        ],
        compiler_params=pltpu.CompilerParams(vmem_limit_bytes=24 << 20),
        cost_estimate=pl.CostEstimate(
            flops=2 * count * SUB * hours, bytes_accessed=6 * count * SUB * hours, transcendentals=0
        ),
        name="scaled_all",
    )(blocks, norm, dep)


def piece_kernel(index_ref, lag_ref, a_ref, halo_ref, b_ref, keep_ref, send_ref, long_ref, shift_ref):
    hours = a_ref.shape[2]
    lags = lag_ref.shape[0]
    long_ref[:, :HALO] = halo_ref[0]
    long_ref[:, HALO:] = a_ref[0]
    lane = lax.broadcasted_iota(jnp.int32, (SUB, LANES), 1)
    for slot in range(lags):
        lag = lag_ref[slot]
        turn = lag & (LANES - 1)
        first = HALO - LANES - (lag - turn)

        def turned(tile):
            start = pl.multiple_of(first + tile * LANES, LANES)
            return pltpu.roll(long_ref[:, pl.ds(start, LANES)], turn, 1)

        before = turned(0)
        for tile in range(hours // LANES):
            here = turned(tile + 1)
            shift_ref[slot * SUB:(slot + 1) * SUB, tile * LANES:(tile + 1) * LANES] = jnp.where(
                lane < turn, before, here
            )
            before = here
    piece = lax.dot_general(
        shift_ref[...], b_ref[0], (((1,), (1,)), ((), ())), preferred_element_type=jnp.float32
    )
    half = lags // 2
    keep_ref[...] = piece[:half * SUB].reshape(half, 1, SUB, SUB)
    send_ref[...] = piece[half * SUB:].reshape(half, 1, SUB, SUB)


def pieces(index, lags, scaled, halo, partner):
    count, _, hours = partner.shape
    half = lags.shape[0] // 2
    out = jax.ShapeDtypeStruct((half, count, SUB, SUB), jnp.float32)
    return pl.pallas_call(
        piece_kernel,
        grid_spec=pltpu.PrefetchScalarGridSpec(
            num_scalar_prefetch=2,
            grid=(count,),
            in_specs=[
                pl.BlockSpec((1, SUB, hours), lambda i, index, lags: (index[i], 0, 0)),
                pl.BlockSpec((1, SUB, HALO), lambda i, index, lags: (index[i], 0, 0)),
                pl.BlockSpec((1, SUB, hours), lambda i, index, lags: (i, 0, 0)),
            ],
            out_specs=[pl.BlockSpec((half, 1, SUB, SUB), lambda i, index, lags: (0, i, 0, 0))] * 2,
            scratch_shapes=[
                pltpu.VMEM((SUB, HALO + hours), jnp.bfloat16),
                pltpu.VMEM((2 * half * SUB, hours), jnp.bfloat16),
            ],
        ),
        out_shape=[out, out],
        compiler_params=pltpu.CompilerParams(vmem_limit_bytes=24 << 20),
        cost_estimate=pl.CostEstimate(
            flops=8 * half * count * SUB * SUB * hours,
            bytes_accessed=count * (4 * SUB * hours + 8 * half * SUB * SUB),
            transcendentals=0,
        ),
        name="pieces",
    )(index, lags, scaled, halo, partner)


def per_device(anomalies, lag_list, pair_plan):
    points, seg_hours = anomalies.shape
    n_grid, n_tm = lax.axis_size("grid"), lax.axis_size("tm")
    all_hours = seg_hours * n_tm
    blocks = anomalies.reshape(points // SUB, SUB, seg_hours)

    def along_grid(value, step):
        return lax.ppermute(value, "grid", [(i, (i + step) % n_grid) for i in range(n_grid)])

    def along_tm(value, target):
        return lax.ppermute(value, "tm", [(i, target(i)) for i in range(n_tm)])

    def ring_near(i):
        return i - i % RING + ((i % RING) ^ 1)

    def ring_far(i):
        return i - i % RING + (RING - 1 - i % RING)

    def other_half(i):
        return (i + RING) % n_tm

    wanted = {k: along_grid(pair_plan[0, k - 1, :, 1], -k) for k in range(1, STEPS + 1)}

    sums = local_sums(anomalies)
    total = sums
    for step in range(1, n_tm):
        total = total + along_tm(sums, lambda i: (i + step) % n_tm)
    total = total.reshape(points // SUB // 4, 2, 4, LANES)
    center = (total[:, 0] / all_hours).reshape(points // SUB, LANES)
    spread = (total[:, 1] / all_hours).reshape(points // SUB, LANES) - center * center
    norm = jnp.stack([center, lax.rsqrt(spread + 1e-05)])

    me = lax.axis_index("tm")
    place, part = me % RING, me // RING
    near, far = place ^ 1, RING - 1 - place
    orders = (
        jnp.stack([place, far, near, RING - 1 - near]),
        jnp.stack([place, near, far, far ^ 1]),
    )
    parts = jnp.stack([part, 1 - part]) * RING
    lag_slots = [jnp.take(lag_list, (order[:, None] + parts[None, :]).reshape(-1)) for order in orders]
    divisor = (all_hours - lag_slots[0][0]).astype(jnp.float32)

    partners = []
    for number, (k, first, count, order) in enumerate(CHUNKS):
        dep = norm if number < IN_FLIGHT else partners[number - IN_FLIGHT]
        picked = scaled_pick(wanted[k][first:first + count], blocks, norm, dep)
        partners.append(along_grid(picked, k))
        if number == 0:
            scaled, tail = scaled_all(blocks, norm, picked)
            halo = lax.ppermute(tail, "tm", [(i, i + 1) for i in range(n_tm - 1)])

    results = {}
    for partner, (k, first, count, order) in zip(partners, CHUNKS):
        keep, send = pieces(
            pair_plan[0, k - 1, first:first + count, 0], lag_slots[order], scaled, halo, partner
        )
        routes = (ring_near, ring_far) if order == 0 else (ring_far, ring_near)
        got_one = along_tm(send, routes[0])
        got_two = along_tm(keep[2:] + got_one[2:], routes[1])
        got_three = along_tm(keep[1] + got_one[1] + got_two[1], other_half)
        results[k, first] = (keep[0] + got_one[0] + got_two[0] + got_three) / divisor
    rows = [
        jnp.concatenate([results[key] for key in sorted(results) if key[0] == k])
        for k in range(1, STEPS + 1)
    ]
    return jnp.stack(rows)[None, :, :, None]


def solution(mesh):
    in_specs = (P("grid", "tm"), P(), P("grid", None, None, None))
    out_specs = P("grid", None, None, "tm", None, None)
    return jax.shard_map(
        per_device, mesh=mesh, in_specs=in_specs, out_specs=out_specs, check_vma=False
    )
```

```python
import functools

import jax
import jax.numpy as jnp
from jax import lax
from jax.experimental import pallas as pl
from jax.experimental.pallas import tpu as pltpu
from jax.sharding import PartitionSpec as P

SUB = 128
LANES = 128
HALO = 256
STEPS = 3
PAIRS = 8
RING = 4
FEW, MANY = 12 << 20, 56 << 20


def sums_kernel(x_ref, out_ref):
    for sub in range(4):
        rows = slice(sub * SUB, (sub + 1) * SUB)
        total = jnp.zeros((SUB, LANES), jnp.float32)
        square = jnp.zeros((SUB, LANES), jnp.float32)
        for tile in range(x_ref.shape[1] // LANES):
            value = x_ref[rows, tile * LANES:(tile + 1) * LANES]
            total = total + value
            square = square + value * value
        total = jnp.sum(total.T, axis=0, keepdims=True)
        square = jnp.sum(square.T, axis=0, keepdims=True)
        for copy in range(out_ref.shape[0]):
            out_ref[copy, sub:sub + 1, :] = total
            out_ref[copy, 4 + sub:5 + sub, :] = square


def local_sums(anomalies, copies):
    points, hours = anomalies.shape
    steps = points // (4 * SUB)
    return pl.pallas_call(
        sums_kernel,
        grid=(steps,),
        in_specs=[pl.BlockSpec((4 * SUB, hours), lambda i: (i, 0))],
        out_specs=pl.BlockSpec((copies, 8, LANES), lambda i: (0, i, 0)),
        out_shape=jax.ShapeDtypeStruct((copies, 8 * steps, LANES), jnp.float32),
        compiler_params=pltpu.CompilerParams(vmem_limit_bytes=MANY),
        cost_estimate=pl.CostEstimate(
            flops=3 * points * hours, bytes_accessed=4 * points * hours, transcendentals=0
        ),
        name="local_sums",
    )(anomalies)


def norm_kernel(hours, sums_ref, norm_ref):
    total = sums_ref[0]
    for part in range(1, sums_ref.shape[0]):
        total = total + sums_ref[part]
    for group in range(total.shape[0] // 8):
        center = total[8 * group:8 * group + 4] / hours
        spread = total[8 * group + 4:8 * group + 8] / hours - center * center
        norm_ref[0, 4 * group:4 * group + 4, :] = center
        norm_ref[1, 4 * group:4 * group + 4, :] = lax.rsqrt(spread + 1e-05)


def norms(sums, hours):
    rows = sums.shape[1] // 2
    return pl.pallas_call(
        functools.partial(norm_kernel, hours),
        out_shape=jax.ShapeDtypeStruct((2, rows, LANES), jnp.float32),
        name="norms",
    )(sums)


def scale_rows(x, center_row, inverse_row, store):
    center = jnp.broadcast_to(center_row, (SUB, LANES)).T
    inverse = jnp.broadcast_to(inverse_row, (SUB, LANES)).T
    for tile in range(x.shape[1] // LANES):
        cols = slice(tile * LANES, (tile + 1) * LANES)
        store(cols, ((x[:, cols] - center) * inverse).astype(jnp.bfloat16))


def scale_kernel(counts, index_ref, x_ref, norm_ref, scaled_ref, tail_ref, *refs):
    send_refs, (wide, narrow, came, went) = refs[:len(counts)], refs[len(counts):]
    subs, _, hours = x_ref.shape

    def arriving(i):
        return pltpu.make_async_copy(x_ref.at[i], wide.at[i], came.at[i])

    for i in range(subs):
        arriving(i).start()
    for i in range(subs):
        arriving(i).wait()

        def store(cols, value):
            narrow[i, :, cols] = value

        scale_rows(wide.at[i], norm_ref[0, i:i + 1, :], norm_ref[1, i:i + 1, :], store)
    leaving = [pltpu.make_async_copy(narrow.at[:, :, hours - HALO:], tail_ref, went.at[0])]
    for send_ref, count in zip(send_refs, counts):
        for i in range(count):
            number = len(leaving)
            leaving.append(
                pltpu.make_async_copy(
                    narrow.at[index_ref[number - 1]], send_ref.at[i], went.at[number]
                )
            )
    leaving.append(pltpu.make_async_copy(narrow, scaled_ref, went.at[len(leaving)]))
    for copy in leaving:
        copy.start()
    for copy in leaving:
        copy.wait()


def scaled_parts(index, counts, blocks, norm):
    subs, _, hours = blocks.shape

    def shape(count, width):
        return jax.ShapeDtypeStruct((count, SUB, width), jnp.bfloat16)

    shapes = [shape(subs, hours), shape(subs, HALO)] + [shape(count, hours) for count in counts]
    return pl.pallas_call(
        functools.partial(scale_kernel, counts),
        in_specs=[
            pl.BlockSpec(memory_space=pltpu.SMEM),
            pl.BlockSpec(memory_space=pl.ANY),
            pl.BlockSpec(memory_space=pltpu.VMEM),
        ],
        out_specs=[pl.BlockSpec(memory_space=pl.ANY)] * len(shapes),
        out_shape=shapes,
        scratch_shapes=[
            pltpu.VMEM((subs, SUB, hours), jnp.float32),
            pltpu.VMEM((subs, SUB, hours), jnp.bfloat16),
            pltpu.SemaphoreType.DMA((subs,)),
            pltpu.SemaphoreType.DMA((sum(counts) + 2,)),
        ],
        compiler_params=pltpu.CompilerParams(vmem_limit_bytes=MANY),
        cost_estimate=pl.CostEstimate(
            flops=2 * subs * SUB * hours, bytes_accessed=10 * subs * SUB * hours, transcendentals=0
        ),
        name="scaled_parts",
    )(index, blocks, norm)


def piece_kernel(index_ref, lag_ref, a_ref, halo_ref, b_ref, *refs):
    keep_ref, send_ref, long_ref, shift_ref = refs[-4:]
    hours = a_ref.shape[2]
    lags = lag_ref.shape[0]
    long_ref[:, :HALO] = halo_ref[0]
    long_ref[:, HALO:] = a_ref[0]
    lane = lax.broadcasted_iota(jnp.int32, (SUB, LANES), 1)
    for slot in range(lags):
        lag = lag_ref[slot]
        turn = lag & (LANES - 1)
        first = HALO - LANES - (lag - turn)

        def turned(tile):
            start = pl.multiple_of(first + tile * LANES, LANES)
            return pltpu.roll(long_ref[:, pl.ds(start, LANES)], turn, 1)

        before = turned(0)
        for tile in range(hours // LANES):
            here = turned(tile + 1)
            shift_ref[slot * SUB:(slot + 1) * SUB, tile * LANES:(tile + 1) * LANES] = jnp.where(
                lane < turn, before, here
            )
            before = here
    piece = lax.dot_general(
        shift_ref[...], b_ref[0], (((1,), (1,)), ((), ())), preferred_element_type=jnp.float32
    )
    half = lags // 2
    keep_ref[...] = piece[:half * SUB].reshape(half, 1, SUB, SUB)
    send_ref[...] = piece[half * SUB:].reshape(half, 1, SUB, SUB)


def pieces(index, lags, scaled, halo, partner, start, deps):
    count, hours = index.shape[0], partner.shape[2]
    half = lags.shape[0] // 2
    out = jax.ShapeDtypeStruct((half, count, SUB, SUB), jnp.float32)
    return pl.pallas_call(
        piece_kernel,
        grid_spec=pltpu.PrefetchScalarGridSpec(
            num_scalar_prefetch=2,
            grid=(count,),
            in_specs=[
                pl.BlockSpec((1, SUB, hours), lambda i, index, lags: (index[i], 0, 0)),
                pl.BlockSpec((1, SUB, HALO), lambda i, index, lags: (index[i], 0, 0)),
                pl.BlockSpec((1, SUB, hours), lambda i, index, lags: (start + i, 0, 0)),
                *[pl.BlockSpec(memory_space=pl.ANY)] * len(deps),
            ],
            out_specs=[pl.BlockSpec((half, 1, SUB, SUB), lambda i, index, lags: (0, i, 0, 0))] * 2,
            scratch_shapes=[
                pltpu.VMEM((SUB, HALO + hours), jnp.bfloat16),
                pltpu.VMEM((2 * half * SUB, hours), jnp.bfloat16),
            ],
        ),
        out_shape=[out, out],
        compiler_params=pltpu.CompilerParams(vmem_limit_bytes=FEW),
        cost_estimate=pl.CostEstimate(
            flops=8 * half * count * SUB * SUB * hours,
            bytes_accessed=count * (4 * SUB * hours + 8 * half * SUB * SUB),
            transcendentals=0,
        ),
        name="pieces",
    )(index, lags, scaled, halo, partner, *deps)


def per_device(anomalies, lag_list, pair_plan):
    points, seg_hours = anomalies.shape
    n_grid, n_tm = lax.axis_size("grid"), lax.axis_size("tm")
    all_hours = seg_hours * n_tm
    blocks = anomalies.reshape(points // SUB, SUB, seg_hours)

    def along_tm(value, target):
        return lax.ppermute(value, "tm", [(i, target(i)) for i in range(n_tm)])

    def ring_near(i):
        return i - i % RING + ((i % RING) ^ 1)

    def ring_far(i):
        return i - i % RING + (RING - 1 - i % RING)

    def other_half(i):
        return (i + RING) % n_tm

    def along_grid(value, route):
        return lax.ppermute(value, "grid", [(i, route(i) % n_grid) for i in range(n_grid)])

    routes = (
        lambda i: i + 3 if i % 2 else i + 1,
        lambda i: i + 2,
        lambda i: i + 1 if i % 2 else i + 3,
    )
    back = (
        lambda i: i - 1 if i % 2 else i - 3,
        lambda i: i - 2,
        lambda i: i - 3 if i % 2 else i - 1,
    )
    even = lax.axis_index("grid") % 2 == 0
    plan = pair_plan[0]
    plans = (jnp.where(even, plan[2], plan[0]), plan[1], jnp.where(even, plan[0], plan[2]))
    wanted = jnp.concatenate([along_grid(one[:, 1], route) for one, route in zip(plans, back)])

    norm = norms(lax.all_to_all(local_sums(anomalies, n_tm), "tm", 0, 0), all_hours)

    me = lax.axis_index("tm")
    place, part = me % RING, me // RING
    near, far = place ^ 1, RING - 1 - place
    orders = (
        jnp.stack([place, far, near, RING - 1 - near]),
        jnp.stack([place, near, far, far ^ 1]),
    )
    parts = jnp.stack([part, 1 - part]) * RING
    lag_slots = [jnp.take(lag_list, (order[:, None] + parts[None, :]).reshape(-1)) for order in orders]
    divisor = (all_hours - lag_slots[0][0]).astype(jnp.float32)

    scaled, tail, *picked = scaled_parts(wanted, (8, 8, 4, 4), blocks, norm)
    halo = lax.ppermute(tail, "tm", [(i, i + 1) for i in range(n_tm - 1)])
    partners = [along_grid(one, routes[which]) for one, which in zip(picked, (0, 1, 2, 2))]

    def summed(which, partner, offset, first, count, deps):
        half = count // 2
        kept, ones, forwards, twos = [], [], [], []
        for order in range(2):
            start = first + order * half
            index = plans[which][start:start + half, 0]
            keep, send = pieces(
                index, lag_slots[order], scaled, halo, partner, start - offset, deps
            )
            kept.append(keep)
            ones.append(along_tm(send, (ring_near, ring_far)[order]))
        for order in range(2):
            forward = kept[order][2:] + ones[order][2:]
            forwards.append(forward)
            twos.append(along_tm(forward, (ring_far, ring_near)[order]))
        across = jnp.concatenate([kept[o][1] + ones[o][1] + twos[o][1] for o in range(2)])
        three = along_tm(across, other_half)
        mine = jnp.concatenate([kept[o][0] + ones[o][0] + twos[o][0] for o in range(2)])
        return (mine + three) / divisor, forwards, kept

    first, deps, _ = summed(0, partners[0], 0, 0, 8, [])
    second, _, deps = summed(1, partners[1], 0, 0, 8, deps)
    third, _, deps = summed(2, partners[2], 0, 0, 4, deps)
    fourth, _, _ = summed(2, partners[3], 4, 4, 4, deps)
    third = jnp.concatenate([third, fourth])
    rows = [jnp.where(even, third, first), second, jnp.where(even, first, third)]
    return jnp.stack(rows)[None, :, :, None]


def solution(mesh):
    in_specs = (P("grid", "tm"), P(), P("grid", None, None, None))
    out_specs = P("grid", None, None, "tm", None, None)
    return jax.shard_map(
        per_device, mesh=mesh, in_specs=in_specs, out_specs=out_specs, check_vma=False
    )
```

```python
import functools

import jax
import jax.numpy as jnp
from jax import lax
from jax.experimental import pallas as pl
from jax.experimental.pallas import tpu as pltpu
from jax.sharding import PartitionSpec as P

SUB = 128
LANES = 128
HALO = 256
STEPS = 3
PAIRS = 8
RING = 4
FEW, MANY = 12 << 20, 56 << 20


def sums_kernel(x_ref, out_ref):
    for sub in range(4):
        rows = slice(sub * SUB, (sub + 1) * SUB)
        total = jnp.zeros((SUB, LANES), jnp.float32)
        square = jnp.zeros((SUB, LANES), jnp.float32)
        for tile in range(x_ref.shape[1] // LANES):
            value = x_ref[rows, tile * LANES:(tile + 1) * LANES]
            total = total + value
            square = square + value * value
        total = jnp.sum(total.T, axis=0, keepdims=True)
        square = jnp.sum(square.T, axis=0, keepdims=True)
        for copy in range(out_ref.shape[0]):
            out_ref[copy, sub:sub + 1, :] = total
            out_ref[copy, 4 + sub:5 + sub, :] = square


def local_sums(anomalies, copies):
    points, hours = anomalies.shape
    steps = points // (4 * SUB)
    return pl.pallas_call(
        sums_kernel,
        grid=(steps,),
        in_specs=[pl.BlockSpec((4 * SUB, hours), lambda i: (i, 0))],
        out_specs=pl.BlockSpec((copies, 8, LANES), lambda i: (0, i, 0)),
        out_shape=jax.ShapeDtypeStruct((copies, 8 * steps, LANES), jnp.float32),
        compiler_params=pltpu.CompilerParams(vmem_limit_bytes=MANY),
        cost_estimate=pl.CostEstimate(
            flops=3 * points * hours, bytes_accessed=4 * points * hours, transcendentals=0
        ),
        name="local_sums",
    )(anomalies)


def norm_kernel(hours, sums_ref, norm_ref):
    total = sums_ref[0]
    for part in range(1, sums_ref.shape[0]):
        total = total + sums_ref[part]
    for group in range(total.shape[0] // 8):
        center = total[8 * group:8 * group + 4] / hours
        spread = total[8 * group + 4:8 * group + 8] / hours - center * center
        norm_ref[0, 4 * group:4 * group + 4, :] = center
        norm_ref[1, 4 * group:4 * group + 4, :] = lax.rsqrt(spread + 1e-05)


def norms(sums, hours):
    rows = sums.shape[1] // 2
    return pl.pallas_call(
        functools.partial(norm_kernel, hours),
        out_shape=jax.ShapeDtypeStruct((2, rows, LANES), jnp.float32),
        name="norms",
    )(sums)


def scale_rows(x, center_row, inverse_row, store):
    center = jnp.broadcast_to(center_row, (SUB, LANES)).T
    inverse = jnp.broadcast_to(inverse_row, (SUB, LANES)).T
    for tile in range(x.shape[1] // LANES):
        cols = slice(tile * LANES, (tile + 1) * LANES)
        store(cols, ((x[:, cols] - center) * inverse).astype(jnp.bfloat16))


def scale_kernel(counts, index_ref, x_ref, norm_ref, scaled_ref, tail_ref, *refs):
    send_refs, (wide, narrow, came, went) = refs[:len(counts)], refs[len(counts):]
    subs, _, hours = x_ref.shape

    def arriving(i):
        return pltpu.make_async_copy(x_ref.at[i], wide.at[i], came.at[i])

    for i in range(subs):
        arriving(i).start()
    for i in range(subs):
        arriving(i).wait()

        def store(cols, value):
            narrow[i, :, cols] = value

        scale_rows(wide.at[i], norm_ref[0, i:i + 1, :], norm_ref[1, i:i + 1, :], store)
    leaving = [pltpu.make_async_copy(narrow.at[:, :, hours - HALO:], tail_ref, went.at[0])]
    for send_ref, count in zip(send_refs, counts):
        for i in range(count):
            number = len(leaving)
            leaving.append(
                pltpu.make_async_copy(
                    narrow.at[index_ref[number - 1]], send_ref.at[i], went.at[number]
                )
            )
    leaving.append(pltpu.make_async_copy(narrow, scaled_ref, went.at[len(leaving)]))
    for copy in leaving:
        copy.start()
    for copy in leaving:
        copy.wait()


def scaled_parts(index, counts, blocks, norm):
    subs, _, hours = blocks.shape

    def shape(count, width):
        return jax.ShapeDtypeStruct((count, SUB, width), jnp.bfloat16)

    shapes = [shape(subs, hours), shape(subs, HALO)] + [shape(count, hours) for count in counts]
    return pl.pallas_call(
        functools.partial(scale_kernel, counts),
        in_specs=[
            pl.BlockSpec(memory_space=pltpu.SMEM),
            pl.BlockSpec(memory_space=pl.ANY),
            pl.BlockSpec(memory_space=pltpu.VMEM),
        ],
        out_specs=[pl.BlockSpec(memory_space=pl.ANY)] * len(shapes),
        out_shape=shapes,
        scratch_shapes=[
            pltpu.VMEM((subs, SUB, hours), jnp.float32),
            pltpu.VMEM((subs, SUB, hours), jnp.bfloat16),
            pltpu.SemaphoreType.DMA((subs,)),
            pltpu.SemaphoreType.DMA((sum(counts) + 2,)),
        ],
        compiler_params=pltpu.CompilerParams(vmem_limit_bytes=MANY),
        cost_estimate=pl.CostEstimate(
            flops=1, bytes_accessed=1, transcendentals=0
        ),
        name="scaled_parts",
    )(index, blocks, norm)


def piece_kernel(index_ref, lag_ref, a_ref, halo_ref, b_ref, *refs):
    keep_ref, send_ref, long_ref, shift_ref = refs[-4:]
    hours = a_ref.shape[2]
    lags = lag_ref.shape[0]
    long_ref[:, :HALO] = halo_ref[0]
    long_ref[:, HALO:] = a_ref[0]
    lane = lax.broadcasted_iota(jnp.int32, (SUB, LANES), 1)
    for slot in range(lags):
        lag = lag_ref[slot]
        turn = lag & (LANES - 1)
        first = HALO - LANES - (lag - turn)

        def turned(tile):
            start = pl.multiple_of(first + tile * LANES, LANES)
            return pltpu.roll(long_ref[:, pl.ds(start, LANES)], turn, 1)

        before = turned(0)
        for tile in range(hours // LANES):
            here = turned(tile + 1)
            shift_ref[slot * SUB:(slot + 1) * SUB, tile * LANES:(tile + 1) * LANES] = jnp.where(
                lane < turn, before, here
            )
            before = here
    piece = lax.dot_general(
        shift_ref[...], b_ref[0], (((1,), (1,)), ((), ())), preferred_element_type=jnp.float32
    )
    half = lags // 2
    keep_ref[...] = piece[:half * SUB].reshape(half, 1, SUB, SUB)
    send_ref[...] = piece[half * SUB:].reshape(half, 1, SUB, SUB)


def pieces(index, lags, scaled, halo, partner, start, deps):
    count, hours = index.shape[0], scaled.shape[2]
    half = lags.shape[0] // 2
    out = jax.ShapeDtypeStruct((half, count, SUB, SUB), jnp.float32)

    return pl.pallas_call(
        piece_kernel,
        grid_spec=pltpu.PrefetchScalarGridSpec(
            num_scalar_prefetch=2,
            grid=(count,),
            in_specs=[
                pl.BlockSpec((1, SUB, hours), lambda i, index, lags: (index[i], 0, 0)),
                pl.BlockSpec((1, SUB, HALO), lambda i, index, lags: (index[i], 0, 0)),
                pl.BlockSpec((1, SUB, hours), lambda i, index, lags: (start + i, 0, 0)),
                *[pl.BlockSpec(memory_space=pl.ANY)] * len(deps),
            ],
            out_specs=[pl.BlockSpec((half, 1, SUB, SUB), lambda i, index, lags: (0, i, 0, 0))] * 2,
            scratch_shapes=[
                pltpu.VMEM((SUB, HALO + hours), jnp.bfloat16),
                pltpu.VMEM((2 * half * SUB, hours), jnp.bfloat16),
            ],
        ),
        out_shape=[out, out],
        compiler_params=pltpu.CompilerParams(vmem_limit_bytes=FEW),
        cost_estimate=pl.CostEstimate(flops=1, bytes_accessed=1, transcendentals=0),
        name="pieces",
    )(index, lags, scaled, halo, partner, *deps)


def tile_call(kernel, name, count, inputs, outputs, scalars=(), deps=()):
    def couple(place):
        return pl.BlockSpec((2, 1, SUB, SUB), lambda i: (place, i, 0, 0))

    return pl.pallas_call(
        kernel,
        grid=(count,),
        in_specs=[
            *[couple(place) for _, place in inputs],
            *[pl.BlockSpec(memory_space=pltpu.SMEM)] * len(scalars),
            *[pl.BlockSpec(memory_space=pl.ANY)] * len(deps),
        ],
        out_specs=[couple(0)] * outputs,
        out_shape=[jax.ShapeDtypeStruct((2, count, SUB, SUB), jnp.float32)] * outputs,
        compiler_params=pltpu.CompilerParams(vmem_limit_bytes=FEW),
        cost_estimate=pl.CostEstimate(flops=1, bytes_accessed=1, transcendentals=0),
        name=name,
    )(*[array for array, _ in inputs], *scalars, *deps)


def forward_kernel(*refs):
    for order in range(2):
        keep_ref, one_ref = refs[2 * order:2 * order + 2]
        refs[order - 2][...] = keep_ref[...] + one_ref[...]


def across_kernel(*refs):
    for order in range(2):
        keep_ref, one_ref, two_ref = refs[3 * order:3 * order + 3]
        total = keep_ref[...] + one_ref[...] + two_ref[...]
        refs[-2][order] = total[0]
        refs[-1][order] = total[1]


def final_kernel(mine_ref, three_ref, divisor_ref, *refs):
    refs[-1][...] = (mine_ref[...] + three_ref[...]) / divisor_ref[0]


def per_device(anomalies, lag_list, pair_plan):
    points, seg_hours = anomalies.shape
    n_grid, n_tm = lax.axis_size("grid"), lax.axis_size("tm")
    all_hours = seg_hours * n_tm
    blocks = anomalies.reshape(points // SUB, SUB, seg_hours)

    def along_tm(value, target):
        return lax.ppermute(value, "tm", [(i, target(i)) for i in range(n_tm)])

    def ring_near(i):
        return i - i % RING + ((i % RING) ^ 1)

    def ring_far(i):
        return i - i % RING + (RING - 1 - i % RING)

    def other_half(i):
        return (i + RING) % n_tm

    def along_grid(value, route):
        return lax.ppermute(value, "grid", [(i, route(i) % n_grid) for i in range(n_grid)])

    routes = (
        lambda i: i + 3 if i % 2 else i + 1,
        lambda i: i + 2,
        lambda i: i + 1 if i % 2 else i + 3,
    )
    back = (
        lambda i: i - 1 if i % 2 else i - 3,
        lambda i: i - 2,
        lambda i: i - 3 if i % 2 else i - 1,
    )
    even = lax.axis_index("grid") % 2 == 0
    plan = pair_plan[0]
    plans = (jnp.where(even, plan[2], plan[0]), plan[1], jnp.where(even, plan[0], plan[2]))
    wanted = jnp.concatenate([along_grid(one[:, 1], route) for one, route in zip(plans, back)])

    norm = norms(lax.all_to_all(local_sums(anomalies, n_tm), "tm", 0, 0), all_hours)

    me = lax.axis_index("tm")
    place, part = me % RING, me // RING
    near, far = place ^ 1, RING - 1 - place
    orders = (
        jnp.stack([place, far, near, RING - 1 - near]),
        jnp.stack([place, near, far, far ^ 1]),
    )
    parts = jnp.stack([part, 1 - part]) * RING
    lag_slots = [jnp.take(lag_list, (order[:, None] + parts[None, :]).reshape(-1)) for order in orders]
    divisor = (all_hours - lag_slots[0][0]).astype(jnp.float32)

    scaled, tail, *picked = scaled_parts(wanted, (8, 8, 8), blocks, norm)
    halo = lax.ppermute(tail, "tm", [(i, i + 1) for i in range(n_tm - 1)])
    beside = along_grid(picked[0], routes[0])
    halo, *picked = lax.optimization_barrier((halo, *picked[1:]))
    over, last = [along_grid(one, route) for one, route in zip(picked, routes[1:])]
    divisor = divisor.reshape(1)

    recent = [scaled]

    def step_one(groups):
        group = []
        for order, (which, first, count, partner, start) in enumerate(groups):
            index = plans[which][first:first + count, 0]
            keep, send = pieces(index, lag_slots[order], scaled, halo, partner, start, recent)
            recent[:] = [keep]
            group.append((keep, along_tm(send, (ring_near, ring_far)[order])))
        return group

    def step_two(group):
        count = group[0][0].shape[1]
        inputs = [(array, 1) for pair in group for array in pair]
        forward = tile_call(forward_kernel, "forward", count, inputs, 2, deps=recent)
        recent[:] = [forward[0]]
        return [
            (*group[order], along_tm(forward[order], (ring_far, ring_near)[order]))
            for order in range(2)
        ]

    def step_three(group):
        count = group[0][0].shape[1]
        inputs = [(array, 0) for triple in group for array in triple]
        mine, across = tile_call(across_kernel, "across", count, inputs, 2, deps=recent)
        recent[:] = [mine]
        return mine, along_tm(across, other_half)

    def step_four(mine, three):
        inputs = [(mine, 0), (three, 0)]
        (out,) = tile_call(
            final_kernel, "final", mine.shape[1], inputs, 1, scalars=[divisor], deps=recent
        )
        recent[:] = [out]
        return out.reshape(-1, SUB, SUB)

    a = step_one([(0, 0, 4, beside, 0), (0, 4, 4, beside, 4)])
    a = step_two(a)
    a = step_three(a)
    b = step_one([(1, 0, 4, over, 0), (1, 4, 4, over, 4)])
    b = step_two(b)
    c = step_one([(2, 0, 2, last, 0), (2, 2, 2, last, 2)])
    b = step_three(b)
    d = step_one([(2, 4, 2, last, 4), (2, 6, 2, last, 6)])
    a = step_four(*a)
    c = step_two(c)
    d = step_two(d)
    b = step_four(*b)
    c = step_three(c)
    d = step_three(d)
    c = step_four(*c)
    d = step_four(*d)
    middle = b
    farthest = jnp.concatenate([c, d])
    rows = [jnp.where(even, farthest, a), middle, jnp.where(even, a, farthest)]
    return jnp.stack(rows)[None, :, :, None]


def solution(mesh):
    in_specs = (P("grid", "tm"), P(), P("grid", None, None, None))
    out_specs = P("grid", None, None, "tm", None, None)
    return jax.shard_map(
        per_device, mesh=mesh, in_specs=in_specs, out_specs=out_specs, check_vma=False
    )
```

```python
import functools

import jax
import jax.numpy as jnp
from jax import lax
from jax.experimental import pallas as pl
from jax.experimental.pallas import tpu as pltpu
from jax.sharding import PartitionSpec as P

SUB = 128
LANES = 128
HALO = 256
SPARE = 40
PACK = 3
STEPS = 3
PAIRS = 8
RING = 4
FEW, MANY = 12 << 20, 56 << 20


def sums_kernel(x_ref, out_ref):
    for sub in range(4):
        rows = slice(sub * SUB, (sub + 1) * SUB)
        total = jnp.zeros((SUB, LANES), jnp.float32)
        square = jnp.zeros((SUB, LANES), jnp.float32)
        for tile in range(x_ref.shape[1] // LANES):
            value = x_ref[rows, tile * LANES:(tile + 1) * LANES]
            total = total + value
            square = square + value * value
        total = jnp.sum(total.T, axis=0, keepdims=True)
        square = jnp.sum(square.T, axis=0, keepdims=True)
        for copy in range(out_ref.shape[0]):
            out_ref[copy, sub:sub + 1, :] = total
            out_ref[copy, 4 + sub:5 + sub, :] = square


def local_sums(anomalies, copies):
    points, hours = anomalies.shape
    steps = points // (4 * SUB)
    return pl.pallas_call(
        sums_kernel,
        grid=(steps,),
        in_specs=[pl.BlockSpec((4 * SUB, hours), lambda i: (i, 0))],
        out_specs=pl.BlockSpec((copies, 8, LANES), lambda i: (0, i, 0)),
        out_shape=jax.ShapeDtypeStruct((copies, 8 * steps, LANES), jnp.float32),
        compiler_params=pltpu.CompilerParams(vmem_limit_bytes=MANY),
        cost_estimate=pl.CostEstimate(
            flops=3 * points * hours, bytes_accessed=4 * points * hours, transcendentals=0
        ),
        name="local_sums",
    )(anomalies)


def norm_kernel(hours, sums_ref, norm_ref):
    total = sums_ref[0]
    for part in range(1, sums_ref.shape[0]):
        total = total + sums_ref[part]
    for group in range(total.shape[0] // 8):
        center = total[8 * group:8 * group + 4] / hours
        spread = total[8 * group + 4:8 * group + 8] / hours - center * center
        norm_ref[0, 4 * group:4 * group + 4, :] = center
        norm_ref[1, 4 * group:4 * group + 4, :] = lax.rsqrt(spread + 1e-05)


def norms(sums, hours):
    rows = sums.shape[1] // 2
    return pl.pallas_call(
        functools.partial(norm_kernel, hours),
        out_shape=jax.ShapeDtypeStruct((2, rows, LANES), jnp.float32),
        name="norms",
    )(sums)


def scale_rows(x, center_row, inverse_row, store):
    center = jnp.broadcast_to(center_row, (SUB, LANES)).T
    inverse = jnp.broadcast_to(inverse_row, (SUB, LANES)).T
    for tile in range(x.shape[1] // LANES):
        cols = slice(tile * LANES, (tile + 1) * LANES)
        store(cols, ((x[:, cols] - center) * inverse).astype(jnp.bfloat16))


def scale_kernel(counts, index_ref, x_ref, norm_ref, scaled_ref, tail_ref, *refs):
    send_refs, (wide, narrow, ends, came, went) = refs[:len(counts)], refs[len(counts):]
    subs, _, hours = x_ref.shape

    def arriving(i):
        return pltpu.make_async_copy(x_ref.at[i], wide.at[i], came.at[i])

    for i in range(subs):
        arriving(i).start()
    for i in range(subs):
        arriving(i).wait()

        def store(cols, value):
            narrow[i, :, cols] = value

        scale_rows(wide.at[i], norm_ref[0, i:i + 1, :], norm_ref[1, i:i + 1, :], store)
    lane = lax.broadcasted_iota(jnp.int32, (SUB, LANES), 1)
    for i in range(subs):
        ends[i] = narrow[i, :, hours - LANES:]
    for group in range(ends.shape[0] - subs):
        tile = jnp.zeros((SUB, LANES), jnp.bfloat16)
        for place in reversed(range(min(PACK, subs - group * PACK))):
            spare = narrow[group * PACK + place, :, hours - HALO:hours - LANES]
            if place:
                spare = pltpu.roll(spare, LANES - place * SPARE, 1)
            tile = jnp.where(lane >= LANES - (place + 1) * SPARE, spare, tile)
        ends[subs + group] = tile
    leaving = [pltpu.make_async_copy(ends, tail_ref, went.at[0])]
    for send_ref, count in zip(send_refs, counts):
        for i in range(count):
            number = len(leaving)
            leaving.append(
                pltpu.make_async_copy(
                    narrow.at[index_ref[number - 1]], send_ref.at[i], went.at[number]
                )
            )
    leaving.append(pltpu.make_async_copy(narrow, scaled_ref, went.at[len(leaving)]))
    for copy in leaving:
        copy.start()
    for copy in leaving:
        copy.wait()


def scaled_parts(index, counts, blocks, norm):
    subs, _, hours = blocks.shape

    tails = subs + pl.cdiv(subs, PACK)

    def shape(count, width):
        return jax.ShapeDtypeStruct((count, SUB, width), jnp.bfloat16)

    shapes = [shape(subs, hours), shape(tails, LANES)] + [shape(count, hours) for count in counts]
    return pl.pallas_call(
        functools.partial(scale_kernel, counts),
        in_specs=[
            pl.BlockSpec(memory_space=pltpu.SMEM),
            pl.BlockSpec(memory_space=pl.ANY),
            pl.BlockSpec(memory_space=pltpu.VMEM),
        ],
        out_specs=[pl.BlockSpec(memory_space=pl.ANY)] * len(shapes),
        out_shape=shapes,
        scratch_shapes=[
            pltpu.VMEM((subs, SUB, hours), jnp.float32),
            pltpu.VMEM((subs, SUB, hours), jnp.bfloat16),
            pltpu.VMEM((tails, SUB, LANES), jnp.bfloat16),
            pltpu.SemaphoreType.DMA((subs,)),
            pltpu.SemaphoreType.DMA((sum(counts) + 2,)),
        ],
        compiler_params=pltpu.CompilerParams(vmem_limit_bytes=MANY),
        cost_estimate=pl.CostEstimate(
            flops=1, bytes_accessed=1, transcendentals=0
        ),
        name="scaled_parts",
    )(index, blocks, norm)


def piece_kernel(index_ref, lag_ref, a_ref, halo_ref, spare_ref, b_ref, *refs):
    keep_ref, send_ref, long_ref, shift_ref = refs[-4:]
    hours = a_ref.shape[2]
    lags = lag_ref.shape[0]
    place = lax.rem(index_ref[pl.program_id(0)], PACK)
    long_ref[:, :LANES] = pltpu.roll(spare_ref[0], place * SPARE, 1)
    long_ref[:, LANES:HALO] = halo_ref[0]
    long_ref[:, HALO:] = a_ref[0]
    lane = lax.broadcasted_iota(jnp.int32, (SUB, LANES), 1)
    for slot in range(lags):
        lag = lag_ref[slot]
        turn = lag & (LANES - 1)
        first = HALO - LANES - (lag - turn)

        def turned(tile):
            start = pl.multiple_of(first + tile * LANES, LANES)
            return pltpu.roll(long_ref[:, pl.ds(start, LANES)], turn, 1)

        before = turned(0)
        for tile in range(hours // LANES):
            here = turned(tile + 1)
            shift_ref[slot * SUB:(slot + 1) * SUB, tile * LANES:(tile + 1) * LANES] = jnp.where(
                lane < turn, before, here
            )
            before = here
    piece = lax.dot_general(
        shift_ref[...], b_ref[0], (((1,), (1,)), ((), ())), preferred_element_type=jnp.float32
    )
    half = lags // 2
    keep_ref[...] = piece[:half * SUB].reshape(half, 1, SUB, SUB)
    send_ref[...] = piece[half * SUB:].reshape(half, 1, SUB, SUB)


def pieces(index, lags, scaled, halo, partner, start, deps):
    count, subs, hours = index.shape[0], scaled.shape[0], scaled.shape[2]
    half = lags.shape[0] // 2
    out = jax.ShapeDtypeStruct((half, count, SUB, SUB), jnp.float32)

    return pl.pallas_call(
        piece_kernel,
        grid_spec=pltpu.PrefetchScalarGridSpec(
            num_scalar_prefetch=2,
            grid=(count,),
            in_specs=[
                pl.BlockSpec((1, SUB, hours), lambda i, index, lags: (index[i], 0, 0)),
                pl.BlockSpec((1, SUB, LANES), lambda i, index, lags: (index[i], 0, 0)),
                pl.BlockSpec(
                    (1, SUB, LANES), lambda i, index, lags: (subs + lax.div(index[i], PACK), 0, 0)
                ),
                pl.BlockSpec((1, SUB, hours), lambda i, index, lags: (start + i, 0, 0)),
                *[pl.BlockSpec(memory_space=pl.ANY)] * len(deps),
            ],
            out_specs=[pl.BlockSpec((half, 1, SUB, SUB), lambda i, index, lags: (0, i, 0, 0))] * 2,
            scratch_shapes=[
                pltpu.VMEM((SUB, HALO + hours), jnp.bfloat16),
                pltpu.VMEM((2 * half * SUB, hours), jnp.bfloat16),
            ],
        ),
        out_shape=[out, out],
        compiler_params=pltpu.CompilerParams(vmem_limit_bytes=FEW),
        cost_estimate=pl.CostEstimate(flops=1, bytes_accessed=1, transcendentals=0),
        name="pieces",
    )(index, lags, scaled, halo, halo, partner, *deps)


def tile_call(kernel, name, count, inputs, outputs, scalars=(), deps=()):
    def couple(place):
        return pl.BlockSpec((2, 1, SUB, SUB), lambda i: (place, i, 0, 0))

    return pl.pallas_call(
        kernel,
        grid=(count,),
        in_specs=[
            *[couple(place) for _, place in inputs],
            *[pl.BlockSpec(memory_space=pltpu.SMEM)] * len(scalars),
            *[pl.BlockSpec(memory_space=pl.ANY)] * len(deps),
        ],
        out_specs=[couple(0)] * outputs,
        out_shape=[jax.ShapeDtypeStruct((2, count, SUB, SUB), jnp.float32)] * outputs,
        compiler_params=pltpu.CompilerParams(vmem_limit_bytes=FEW),
        cost_estimate=pl.CostEstimate(flops=1, bytes_accessed=1, transcendentals=0),
        name=name,
    )(*[array for array, _ in inputs], *scalars, *deps)


def forward_kernel(keep_ref, one_ref, *refs):
    refs[-1][...] = keep_ref[...] + one_ref[...]


def across_kernel(*refs):
    for order in range(2):
        keep_ref, one_ref, two_ref = refs[3 * order:3 * order + 3]
        total = keep_ref[...] + one_ref[...] + two_ref[...]
        refs[-2][order] = total[0]
        refs[-1][order] = total[1]


def final_kernel(mine_ref, three_ref, divisor_ref, *refs):
    refs[-1][...] = (mine_ref[...] + three_ref[...]) / divisor_ref[0]


def per_device(anomalies, lag_list, pair_plan):
    points, seg_hours = anomalies.shape
    n_grid, n_tm = lax.axis_size("grid"), lax.axis_size("tm")
    all_hours = seg_hours * n_tm
    blocks = anomalies.reshape(points // SUB, SUB, seg_hours)

    def along_tm(value, target):
        return lax.ppermute(value, "tm", [(i, target(i)) for i in range(n_tm)])

    def ring_near(i):
        return i - i % RING + ((i % RING) ^ 1)

    def ring_far(i):
        return i - i % RING + (RING - 1 - i % RING)

    def other_half(i):
        return (i + RING) % n_tm

    def along_grid(value, route):
        return lax.ppermute(value, "grid", [(i, route(i) % n_grid) for i in range(n_grid)])

    routes = (
        lambda i: i + 3 if i % 2 else i + 1,
        lambda i: i + 2,
        lambda i: i + 1 if i % 2 else i + 3,
    )
    back = (
        lambda i: i - 1 if i % 2 else i - 3,
        lambda i: i - 2,
        lambda i: i - 3 if i % 2 else i - 1,
    )
    even = lax.axis_index("grid") % 2 == 0
    plan = pair_plan[0]
    plans = (jnp.where(even, plan[2], plan[0]), plan[1], jnp.where(even, plan[0], plan[2]))
    sums, *seconds = lax.optimization_barrier(
        (local_sums(anomalies, n_tm), *[one[:, 1] for one in plans])
    )
    wanted = jnp.concatenate([along_grid(one, route) for one, route in zip(seconds, back)])
    norm = norms(lax.all_to_all(sums, "tm", 0, 0), all_hours)

    me = lax.axis_index("tm")
    place, part = me % RING, me // RING
    near, far = place ^ 1, RING - 1 - place
    orders = (
        jnp.stack([place, far, near, RING - 1 - near]),
        jnp.stack([place, near, far, far ^ 1]),
    )
    parts = jnp.stack([part, 1 - part]) * RING
    lag_slots = [jnp.take(lag_list, (order[:, None] + parts[None, :]).reshape(-1)) for order in orders]
    divisor = (all_hours - lag_slots[0][0]).astype(jnp.float32)

    scaled, tail, *picked = scaled_parts(wanted, (4, 4, 8, 4, 4), blocks, norm)
    halo = lax.ppermute(tail, "tm", [(i, i + 1) for i in range(n_tm - 1)])
    beside = along_grid(picked[0], routes[0])
    beside, waiting = lax.optimization_barrier((beside, picked[1]))
    beside = [beside, along_grid(waiting, routes[0])]
    halo, waiting = lax.optimization_barrier((halo, picked[2]))
    over = along_grid(waiting, routes[1])
    divisor = divisor.reshape(1)

    recent = [scaled]

    def step_one(groups, orders=(0, 1)):
        group = []
        for order, (which, first, count, partner, start) in zip(orders, groups):
            index = plans[which][first:first + count, 0]
            keep, send = pieces(index, lag_slots[order], scaled, halo, partner, start, recent)
            recent[:] = [keep]
            group.append((keep, along_tm(send, (ring_near, ring_far)[order])))
        return group

    def step_two(group):
        result = []
        for order, (keep, one) in enumerate(group):
            inputs = [(keep, 1), (one, 1)]
            (forward,) = tile_call(
                forward_kernel, "forward", keep.shape[1], inputs, 1, deps=recent
            )
            recent[:] = [forward]
            result.append((keep, one, along_tm(forward, (ring_far, ring_near)[order])))
        return result

    def step_three(group):
        count = group[0][0].shape[1]
        inputs = [(array, 0) for triple in group for array in triple]
        mine, across = tile_call(across_kernel, "across", count, inputs, 2, deps=recent)
        recent[:] = [mine]
        return mine, along_tm(across, other_half)

    def step_four(mine, three):
        inputs = [(mine, 0), (three, 0)]
        (out,) = tile_call(
            final_kernel, "final", mine.shape[1], inputs, 1, scalars=[divisor], deps=recent
        )
        recent[:] = [out]
        return out.reshape(-1, SUB, SUB)

    a = step_one([(0, 0, 4, beside[0], 0), (0, 4, 4, beside[1], 0)])
    a = step_two(a)
    recent[0], *waiting = lax.optimization_barrier((recent[0], *picked[3:]))
    last = [along_grid(one, routes[2]) for one in waiting]
    b = step_one([(1, 0, 4, over, 0)], (0,))
    a = step_three(a)
    b += step_one([(1, 4, 4, over, 4)], (1,))
    c = step_one([(2, 0, 2, last[0], 0), (2, 2, 2, last[0], 2)])
    b = step_two(b)
    d = step_one([(2, 4, 2, last[1], 0), (2, 6, 2, last[1], 2)])
    c = step_two(c)
    b = step_three(b)
    d = step_two(d)
    c = step_three(c)
    a = step_four(*a)
    b = step_four(*b)
    d = step_three(d)
    c = step_four(*c)
    d = step_four(*d)
    middle = b
    farthest = jnp.concatenate([c, d])
    rows = [jnp.where(even, farthest, a), middle, jnp.where(even, a, farthest)]
    return jnp.stack(rows)[None, :, :, None]


def solution(mesh):
    in_specs = (P("grid", "tm"), P(), P("grid", None, None, None))
    out_specs = P("grid", None, None, "tm", None, None)
    return jax.shard_map(
        per_device, mesh=mesh, in_specs=in_specs, out_specs=out_specs, check_vma=False
    )
```

```python
import functools

import jax
import jax.numpy as jnp
from jax import lax
from jax.experimental import pallas as pl
from jax.experimental.pallas import tpu as pltpu
from jax.sharding import PartitionSpec as P

SUB = 128
LANES = 128
HALO = 256
SPARE = 40
PACK = 3
STEPS = 3
PAIRS = 8
RING = 4
FEW, MANY = 12 << 20, 56 << 20


def sums_kernel(x_ref, out_ref):
    for sub in range(4):
        rows = slice(sub * SUB, (sub + 1) * SUB)
        total = jnp.zeros((SUB, LANES), jnp.float32)
        square = jnp.zeros((SUB, LANES), jnp.float32)
        for tile in range(x_ref.shape[1] // LANES):
            value = x_ref[rows, tile * LANES:(tile + 1) * LANES]
            total = total + value
            square = square + value * value
        total = jnp.sum(total.T, axis=0, keepdims=True)
        square = jnp.sum(square.T, axis=0, keepdims=True)
        for copy in range(out_ref.shape[0]):
            out_ref[copy, sub:sub + 1, :] = total
            out_ref[copy, 4 + sub:5 + sub, :] = square


def local_sums(anomalies, copies):
    points, hours = anomalies.shape
    steps = points // (4 * SUB)
    return pl.pallas_call(
        sums_kernel,
        grid=(steps,),
        in_specs=[pl.BlockSpec((4 * SUB, hours), lambda i: (i, 0))],
        out_specs=pl.BlockSpec((copies, 8, LANES), lambda i: (0, i, 0)),
        out_shape=jax.ShapeDtypeStruct((copies, 8 * steps, LANES), jnp.float32),
        compiler_params=pltpu.CompilerParams(vmem_limit_bytes=MANY),
        cost_estimate=pl.CostEstimate(
            flops=3 * points * hours, bytes_accessed=4 * points * hours, transcendentals=0
        ),
        name="local_sums",
    )(anomalies)


def norm_kernel(hours, sums_ref, norm_ref):
    total = sums_ref[0]
    for part in range(1, sums_ref.shape[0]):
        total = total + sums_ref[part]
    for group in range(total.shape[0] // 8):
        center = total[8 * group:8 * group + 4] / hours
        spread = total[8 * group + 4:8 * group + 8] / hours - center * center
        norm_ref[0, 4 * group:4 * group + 4, :] = center
        norm_ref[1, 4 * group:4 * group + 4, :] = lax.rsqrt(spread + 1e-05)


def norms(sums, hours):
    rows = sums.shape[1] // 2
    return pl.pallas_call(
        functools.partial(norm_kernel, hours),
        out_shape=jax.ShapeDtypeStruct((2, rows, LANES), jnp.float32),
        name="norms",
    )(sums)


def scale_rows(x, center_row, inverse_row, store):
    center = jnp.broadcast_to(center_row, (SUB, LANES)).T
    inverse = jnp.broadcast_to(inverse_row, (SUB, LANES)).T
    for tile in range(x.shape[1] // LANES):
        cols = slice(tile * LANES, (tile + 1) * LANES)
        store(cols, ((x[:, cols] - center) * inverse).astype(jnp.bfloat16))


def scale_kernel(counts, index_ref, x_ref, norm_ref, scaled_ref, tail_ref, *refs):
    send_refs, (wide, narrow, ends, came, went, stays) = refs[:len(counts)], refs[len(counts):]
    subs, _, hours = x_ref.shape

    def arriving(i):
        return pltpu.make_async_copy(x_ref.at[i], wide.at[i], came.at[i])

    for i in range(subs):
        arriving(i).start()
    for i in range(subs):
        arriving(i).wait()

        def store(cols, value):
            narrow[i, :, cols] = value

        scale_rows(wide.at[i], norm_ref[0, i:i + 1, :], norm_ref[1, i:i + 1, :], store)
        kept = pltpu.make_async_copy(narrow.at[i], scaled_ref.at[i], stays.at[i])
        kept.start()
    lane = lax.broadcasted_iota(jnp.int32, (SUB, LANES), 1)
    for i in range(subs):
        ends[i] = narrow[i, :, hours - LANES:]
    for group in range(ends.shape[0] - subs):
        tile = jnp.zeros((SUB, LANES), jnp.bfloat16)
        for place in reversed(range(min(PACK, subs - group * PACK))):
            spare = narrow[group * PACK + place, :, hours - HALO:hours - LANES]
            if place:
                spare = pltpu.roll(spare, LANES - place * SPARE, 1)
            tile = jnp.where(lane >= LANES - (place + 1) * SPARE, spare, tile)
        ends[subs + group] = tile
    leaving = [pltpu.make_async_copy(ends, tail_ref, went.at[0])]
    for send_ref, count in zip(send_refs, counts):
        for i in range(count):
            number = len(leaving)
            leaving.append(
                pltpu.make_async_copy(
                    narrow.at[index_ref[number - 1]], send_ref.at[i], went.at[number]
                )
            )
    for copy in leaving:
        copy.start()
    for copy in leaving:
        copy.wait()
    for i in range(subs):
        pltpu.make_async_copy(narrow.at[i], scaled_ref.at[i], stays.at[i]).wait()


def scaled_parts(index, counts, blocks, norm):
    subs, _, hours = blocks.shape

    tails = subs + pl.cdiv(subs, PACK)

    def shape(count, width):
        return jax.ShapeDtypeStruct((count, SUB, width), jnp.bfloat16)

    shapes = [shape(subs, hours), shape(tails, LANES)] + [shape(count, hours) for count in counts]
    return pl.pallas_call(
        functools.partial(scale_kernel, counts),
        in_specs=[
            pl.BlockSpec(memory_space=pltpu.SMEM),
            pl.BlockSpec(memory_space=pl.ANY),
            pl.BlockSpec(memory_space=pltpu.VMEM),
        ],
        out_specs=[pl.BlockSpec(memory_space=pl.ANY)] * len(shapes),
        out_shape=shapes,
        scratch_shapes=[
            pltpu.VMEM((subs, SUB, hours), jnp.float32),
            pltpu.VMEM((subs, SUB, hours), jnp.bfloat16),
            pltpu.VMEM((tails, SUB, LANES), jnp.bfloat16),
            pltpu.SemaphoreType.DMA((subs,)),
            pltpu.SemaphoreType.DMA((sum(counts) + 1,)),
            pltpu.SemaphoreType.DMA((subs,)),
        ],
        compiler_params=pltpu.CompilerParams(vmem_limit_bytes=MANY),
        cost_estimate=pl.CostEstimate(
            flops=1, bytes_accessed=1, transcendentals=0
        ),
        name="scaled_parts",
    )(index, blocks, norm)


def piece_kernel(index_ref, lag_ref, a_ref, halo_ref, spare_ref, b_ref, *refs):
    keep_ref, send_ref, long_ref, shift_ref = refs[-4:]
    hours = a_ref.shape[2]
    lags = lag_ref.shape[0]
    place = lax.rem(index_ref[pl.program_id(0)], PACK)
    long_ref[:, :LANES] = pltpu.roll(spare_ref[0], place * SPARE, 1)
    long_ref[:, LANES:HALO] = halo_ref[0]
    long_ref[:, HALO:] = a_ref[0]
    lane = lax.broadcasted_iota(jnp.int32, (SUB, LANES), 1)
    for slot in range(lags):
        lag = lag_ref[slot]
        turn = lag & (LANES - 1)
        first = HALO - LANES - (lag - turn)

        def turned(tile):
            start = pl.multiple_of(first + tile * LANES, LANES)
            return pltpu.roll(long_ref[:, pl.ds(start, LANES)], turn, 1)

        before = turned(0)
        for tile in range(hours // LANES):
            here = turned(tile + 1)
            shift_ref[slot * SUB:(slot + 1) * SUB, tile * LANES:(tile + 1) * LANES] = jnp.where(
                lane < turn, before, here
            )
            before = here
    piece = lax.dot_general(
        shift_ref[...], b_ref[0], (((1,), (1,)), ((), ())), preferred_element_type=jnp.float32
    )
    half = lags // 2
    keep_ref[...] = piece[:half * SUB].reshape(half, 1, SUB, SUB)
    send_ref[...] = piece[half * SUB:].reshape(half, 1, SUB, SUB)


def pieces(index, lags, scaled, halo, partner, start, deps):
    count, subs, hours = index.shape[0], scaled.shape[0], scaled.shape[2]
    half = lags.shape[0] // 2
    out = jax.ShapeDtypeStruct((half, count, SUB, SUB), jnp.float32)

    return pl.pallas_call(
        piece_kernel,
        grid_spec=pltpu.PrefetchScalarGridSpec(
            num_scalar_prefetch=2,
            grid=(count,),
            in_specs=[
                pl.BlockSpec((1, SUB, hours), lambda i, index, lags: (index[i], 0, 0)),
                pl.BlockSpec((1, SUB, LANES), lambda i, index, lags: (index[i], 0, 0)),
                pl.BlockSpec(
                    (1, SUB, LANES), lambda i, index, lags: (subs + lax.div(index[i], PACK), 0, 0)
                ),
                pl.BlockSpec((1, SUB, hours), lambda i, index, lags: (start + i, 0, 0)),
                *[pl.BlockSpec(memory_space=pl.ANY)] * len(deps),
            ],
            out_specs=[pl.BlockSpec((half, 1, SUB, SUB), lambda i, index, lags: (0, i, 0, 0))] * 2,
            scratch_shapes=[
                pltpu.VMEM((SUB, HALO + hours), jnp.bfloat16),
                pltpu.VMEM((2 * half * SUB, hours), jnp.bfloat16),
            ],
        ),
        out_shape=[out, out],
        compiler_params=pltpu.CompilerParams(vmem_limit_bytes=FEW),
        cost_estimate=pl.CostEstimate(flops=1, bytes_accessed=1, transcendentals=0),
        name="pieces",
    )(index, lags, scaled, halo, halo, partner, *deps)


def tile_call(kernel, name, count, inputs, outputs, scalars=(), deps=()):
    def couple(place):
        return pl.BlockSpec((2, 1, SUB, SUB), lambda i: (place, i, 0, 0))

    return pl.pallas_call(
        kernel,
        grid=(count,),
        in_specs=[
            *[couple(place) for _, place in inputs],
            *[pl.BlockSpec(memory_space=pltpu.SMEM)] * len(scalars),
            *[pl.BlockSpec(memory_space=pl.ANY)] * len(deps),
        ],
        out_specs=[couple(0)] * outputs,
        out_shape=[jax.ShapeDtypeStruct((2, count, SUB, SUB), jnp.float32)] * outputs,
        compiler_params=pltpu.CompilerParams(vmem_limit_bytes=FEW),
        cost_estimate=pl.CostEstimate(flops=1, bytes_accessed=1, transcendentals=0),
        name=name,
    )(*[array for array, _ in inputs], *scalars, *deps)


def forward_kernel(keep_ref, one_ref, *refs):
    refs[-1][...] = keep_ref[...] + one_ref[...]


def across_kernel(*refs):
    for order in range(2):
        keep_ref, one_ref, two_ref = refs[3 * order:3 * order + 3]
        total = keep_ref[...] + one_ref[...] + two_ref[...]
        refs[-2][order] = total[0]
        refs[-1][order] = total[1]


def final_kernel(mine_ref, three_ref, divisor_ref, *refs):
    refs[-1][...] = (mine_ref[...] + three_ref[...]) / divisor_ref[0]


def per_device(anomalies, lag_list, pair_plan):
    points, seg_hours = anomalies.shape
    n_grid, n_tm = lax.axis_size("grid"), lax.axis_size("tm")
    all_hours = seg_hours * n_tm
    blocks = anomalies.reshape(points // SUB, SUB, seg_hours)

    def along_tm(value, target):
        return lax.ppermute(value, "tm", [(i, target(i)) for i in range(n_tm)])

    def ring_near(i):
        return i - i % RING + ((i % RING) ^ 1)

    def ring_far(i):
        return i - i % RING + (RING - 1 - i % RING)

    def other_half(i):
        return (i + RING) % n_tm

    def along_grid(value, route):
        return lax.ppermute(value, "grid", [(i, route(i) % n_grid) for i in range(n_grid)])

    routes = (
        lambda i: i + 3 if i % 2 else i + 1,
        lambda i: i + 2,
        lambda i: i + 1 if i % 2 else i + 3,
    )
    back = (
        lambda i: i - 1 if i % 2 else i - 3,
        lambda i: i - 2,
        lambda i: i - 3 if i % 2 else i - 1,
    )
    even = lax.axis_index("grid") % 2 == 0
    plan = pair_plan[0]
    plans = (jnp.where(even, plan[2], plan[0]), plan[1], jnp.where(even, plan[0], plan[2]))
    sums, *seconds = lax.optimization_barrier(
        (local_sums(anomalies, n_tm), *[one[:, 1] for one in plans])
    )
    wanted = jnp.concatenate([along_grid(one, route) for one, route in zip(seconds, back)])
    norm = norms(lax.all_to_all(sums, "tm", 0, 0), all_hours)

    me = lax.axis_index("tm")
    place, part = me % RING, me // RING
    near, far = place ^ 1, RING - 1 - place
    orders = (
        jnp.stack([place, far, near, RING - 1 - near]),
        jnp.stack([place, near, far, far ^ 1]),
    )
    parts = jnp.stack([part, 1 - part]) * RING
    lag_slots = [jnp.take(lag_list, (order[:, None] + parts[None, :]).reshape(-1)) for order in orders]
    divisor = (all_hours - lag_slots[0][0]).astype(jnp.float32)

    scaled, tail, *picked = scaled_parts(wanted, (4, 4, 8, 4, 4), blocks, norm)
    halo = lax.ppermute(tail, "tm", [(i, i + 1) for i in range(n_tm - 1)])
    beside = along_grid(picked[0], routes[0])
    beside, waiting = lax.optimization_barrier((beside, picked[1]))
    beside = [beside, along_grid(waiting, routes[0])]
    halo, waiting = lax.optimization_barrier((halo, picked[2]))
    over = along_grid(waiting, routes[1])
    divisor = divisor.reshape(1)

    recent = [scaled]

    def step_one(groups, orders=(0, 1)):
        group = []
        for order, (which, first, count, partner, start) in zip(orders, groups):
            index = plans[which][first:first + count, 0]
            keep, send = pieces(index, lag_slots[order], scaled, halo, partner, start, recent)
            recent[:] = [keep]
            group.append((keep, along_tm(send, (ring_near, ring_far)[order])))
        return group

    def step_two(group):
        result = []
        for order, (keep, one) in enumerate(group):
            inputs = [(keep, 1), (one, 1)]
            (forward,) = tile_call(
                forward_kernel, "forward", keep.shape[1], inputs, 1, deps=recent
            )
            recent[:] = [forward]
            result.append((keep, one, along_tm(forward, (ring_far, ring_near)[order])))
        return result

    def step_three(group):
        count = group[0][0].shape[1]
        inputs = [(array, 0) for triple in group for array in triple]
        mine, across = tile_call(across_kernel, "across", count, inputs, 2, deps=recent)
        recent[:] = [mine]
        return mine, along_tm(across, other_half)

    def step_four(mine, three):
        inputs = [(mine, 0), (three, 0)]
        (out,) = tile_call(
            final_kernel, "final", mine.shape[1], inputs, 1, scalars=[divisor], deps=recent
        )
        recent[:] = [out]
        return out.reshape(-1, SUB, SUB)

    a = step_one([(0, 0, 4, beside[0], 0), (0, 4, 4, beside[1], 0)])
    a = step_two(a)
    recent[0], *waiting = lax.optimization_barrier((recent[0], *picked[3:]))
    last = [along_grid(one, routes[2]) for one in waiting]
    b = step_one([(1, 0, 4, over, 0)], (0,))
    a = step_three(a)
    b += step_one([(1, 4, 4, over, 4)], (1,))
    c = step_one([(2, 0, 2, last[0], 0), (2, 2, 2, last[0], 2)])
    b = step_two(b)
    d = step_one([(2, 4, 2, last[1], 0), (2, 6, 2, last[1], 2)])
    c = step_two(c)
    b = step_three(b)
    d = step_two(d)
    c = step_three(c)
    a = step_four(*a)
    b = step_four(*b)
    d = step_three(d)
    c = step_four(*c)
    d = step_four(*d)
    middle = b
    farthest = jnp.concatenate([c, d])
    rows = [jnp.where(even, farthest, a), middle, jnp.where(even, a, farthest)]
    return jnp.stack(rows)[None, :, :, None]


def solution(mesh):
    in_specs = (P("grid", "tm"), P(), P("grid", None, None, None))
    out_specs = P("grid", None, None, "tm", None, None)
    return jax.shard_map(
        per_device, mesh=mesh, in_specs=in_specs, out_specs=out_specs, check_vma=False
    )
```

```python
import functools

import jax
import jax.numpy as jnp
from jax import lax
from jax.experimental import pallas as pl
from jax.experimental.pallas import tpu as pltpu
from jax.sharding import PartitionSpec as P

SUB = 128
LANES = 128
HALO = 256
SPARE = 40
PACK = 3
STEPS = 3
PAIRS = 8
RING = 4
FEW, MANY = 12 << 20, 56 << 20


def sums_kernel(x_ref, out_ref):
    for sub in range(4):
        rows = slice(sub * SUB, (sub + 1) * SUB)
        total = jnp.zeros((SUB, LANES), jnp.float32)
        square = jnp.zeros((SUB, LANES), jnp.float32)
        for tile in range(x_ref.shape[1] // LANES):
            value = x_ref[rows, tile * LANES:(tile + 1) * LANES]
            total = total + value
            square = square + value * value
        total = jnp.sum(total.T, axis=0, keepdims=True)
        square = jnp.sum(square.T, axis=0, keepdims=True)
        for copy in range(out_ref.shape[0]):
            out_ref[copy, sub:sub + 1, :] = total
            out_ref[copy, 4 + sub:5 + sub, :] = square


def local_sums(anomalies, copies):
    points, hours = anomalies.shape
    steps = points // (4 * SUB)
    return pl.pallas_call(
        sums_kernel,
        grid=(steps,),
        in_specs=[pl.BlockSpec((4 * SUB, hours), lambda i: (i, 0))],
        out_specs=pl.BlockSpec((copies, 8, LANES), lambda i: (0, i, 0)),
        out_shape=jax.ShapeDtypeStruct((copies, 8 * steps, LANES), jnp.float32),
        compiler_params=pltpu.CompilerParams(vmem_limit_bytes=MANY),
        cost_estimate=pl.CostEstimate(
            flops=3 * points * hours, bytes_accessed=4 * points * hours, transcendentals=0
        ),
        name="local_sums",
    )(anomalies)


def norm_kernel(hours, sums_ref, norm_ref):
    total = sums_ref[0]
    for part in range(1, sums_ref.shape[0]):
        total = total + sums_ref[part]
    for group in range(total.shape[0] // 8):
        center = total[8 * group:8 * group + 4] / hours
        spread = total[8 * group + 4:8 * group + 8] / hours - center * center
        norm_ref[0, 4 * group:4 * group + 4, :] = center
        norm_ref[1, 4 * group:4 * group + 4, :] = lax.rsqrt(spread + 1e-05)


def norms(sums, hours):
    rows = sums.shape[1] // 2
    return pl.pallas_call(
        functools.partial(norm_kernel, hours),
        out_shape=jax.ShapeDtypeStruct((2, rows, LANES), jnp.float32),
        name="norms",
    )(sums)


def scale_rows(x, center_row, inverse_row, store):
    center = jnp.broadcast_to(center_row, (SUB, LANES)).T
    inverse = jnp.broadcast_to(inverse_row, (SUB, LANES)).T
    for tile in range(x.shape[1] // LANES):
        cols = slice(tile * LANES, (tile + 1) * LANES)
        store(cols, ((x[:, cols] - center) * inverse).astype(jnp.bfloat16))


def scale_kernel(counts, index_ref, x_ref, norm_ref, scaled_ref, tail_ref, *refs):
    send_refs, (wide, narrow, ends, came, went, stays) = refs[:len(counts)], refs[len(counts):]
    subs, _, hours = x_ref.shape

    def arriving(i):
        return pltpu.make_async_copy(x_ref.at[i], wide.at[i], came.at[i])

    for i in range(subs):
        arriving(i).start()
    for i in range(subs):
        arriving(i).wait()

        def store(cols, value):
            narrow[i, :, cols] = value

        scale_rows(wide.at[i], norm_ref[0, i:i + 1, :], norm_ref[1, i:i + 1, :], store)
        kept = pltpu.make_async_copy(narrow.at[i], scaled_ref.at[i], stays.at[i])
        kept.start()
    lane = lax.broadcasted_iota(jnp.int32, (SUB, LANES), 1)
    for i in range(subs):
        ends[i] = narrow[i, :, hours - LANES:]
    for group in range(ends.shape[0] - subs):
        tile = jnp.zeros((SUB, LANES), jnp.bfloat16)
        for place in reversed(range(min(PACK, subs - group * PACK))):
            spare = narrow[group * PACK + place, :, hours - HALO:hours - LANES]
            if place:
                spare = pltpu.roll(spare, LANES - place * SPARE, 1)
            tile = jnp.where(lane >= LANES - (place + 1) * SPARE, spare, tile)
        ends[subs + group] = tile
    leaving = [pltpu.make_async_copy(ends, tail_ref, went.at[0])]
    for send_ref, count in zip(send_refs, counts):
        for i in range(count):
            number = len(leaving)
            leaving.append(
                pltpu.make_async_copy(
                    narrow.at[index_ref[number - 1]], send_ref.at[i], went.at[number]
                )
            )
    for copy in leaving:
        copy.start()
    for copy in leaving:
        copy.wait()
    for i in range(subs):
        pltpu.make_async_copy(narrow.at[i], scaled_ref.at[i], stays.at[i]).wait()


def scaled_parts(index, counts, blocks, norm):
    subs, _, hours = blocks.shape

    tails = subs + pl.cdiv(subs, PACK)

    def shape(count, width):
        return jax.ShapeDtypeStruct((count, SUB, width), jnp.bfloat16)

    shapes = [shape(subs, hours), shape(tails, LANES)] + [shape(count, hours) for count in counts]
    return pl.pallas_call(
        functools.partial(scale_kernel, counts),
        in_specs=[
            pl.BlockSpec(memory_space=pltpu.SMEM),
            pl.BlockSpec(memory_space=pl.ANY),
            pl.BlockSpec(memory_space=pltpu.VMEM),
        ],
        out_specs=[pl.BlockSpec(memory_space=pl.ANY)] * len(shapes),
        out_shape=shapes,
        scratch_shapes=[
            pltpu.VMEM((subs, SUB, hours), jnp.float32),
            pltpu.VMEM((subs, SUB, hours), jnp.bfloat16),
            pltpu.VMEM((tails, SUB, LANES), jnp.bfloat16),
            pltpu.SemaphoreType.DMA((subs,)),
            pltpu.SemaphoreType.DMA((sum(counts) + 1,)),
            pltpu.SemaphoreType.DMA((subs,)),
        ],
        compiler_params=pltpu.CompilerParams(vmem_limit_bytes=MANY),
        cost_estimate=pl.CostEstimate(
            flops=1, bytes_accessed=1, transcendentals=0
        ),
        name="scaled_parts",
    )(index, blocks, norm)


def rows_kernel(counts, start, index_ref, scaled_ref, *refs):
    send_refs, (held, came, went) = refs[:len(counts)], refs[len(counts):]
    places = [send_ref.at[i] for send_ref, count in zip(send_refs, counts) for i in range(count)]

    def arriving(i):
        return pltpu.make_async_copy(scaled_ref.at[index_ref[start + i]], held.at[i], came.at[i])

    def leaving(i):
        return pltpu.make_async_copy(held.at[i], places[i], went.at[i])

    for i in range(len(places)):
        arriving(i).start()
    for i in range(len(places)):
        arriving(i).wait()
        leaving(i).start()
    for i in range(len(places)):
        leaving(i).wait()


def picked_rows(index, counts, start, scaled):
    shapes = [jax.ShapeDtypeStruct((count,) + scaled.shape[1:], scaled.dtype) for count in counts]
    return pl.pallas_call(
        functools.partial(rows_kernel, counts, start),
        in_specs=[pl.BlockSpec(memory_space=pltpu.SMEM), pl.BlockSpec(memory_space=pl.ANY)],
        out_specs=[pl.BlockSpec(memory_space=pl.ANY)] * len(shapes),
        out_shape=shapes,
        scratch_shapes=[
            pltpu.VMEM((sum(counts),) + scaled.shape[1:], scaled.dtype),
            pltpu.SemaphoreType.DMA((sum(counts),)),
            pltpu.SemaphoreType.DMA((sum(counts),)),
        ],
        compiler_params=pltpu.CompilerParams(vmem_limit_bytes=MANY),
        cost_estimate=pl.CostEstimate(flops=1, bytes_accessed=1, transcendentals=0),
        name="picked_rows",
    )(index, scaled)


def piece_kernel(index_ref, lag_ref, a_ref, halo_ref, spare_ref, b_ref, *refs):
    keep_ref, send_ref, long_ref, shift_ref = refs[-4:]
    hours = a_ref.shape[2]
    lags = lag_ref.shape[0]
    place = lax.rem(index_ref[pl.program_id(0)], PACK)
    long_ref[:, :LANES] = pltpu.roll(spare_ref[0], place * SPARE, 1)
    long_ref[:, LANES:HALO] = halo_ref[0]
    long_ref[:, HALO:] = a_ref[0]
    lane = lax.broadcasted_iota(jnp.int32, (SUB, LANES), 1)
    for slot in range(lags):
        lag = lag_ref[slot]
        turn = lag & (LANES - 1)
        first = HALO - LANES - (lag - turn)

        def turned(tile):
            start = pl.multiple_of(first + tile * LANES, LANES)
            return pltpu.roll(long_ref[:, pl.ds(start, LANES)], turn, 1)

        before = turned(0)
        for tile in range(hours // LANES):
            here = turned(tile + 1)
            shift_ref[slot * SUB:(slot + 1) * SUB, tile * LANES:(tile + 1) * LANES] = jnp.where(
                lane < turn, before, here
            )
            before = here
    piece = lax.dot_general(
        shift_ref[...], b_ref[0], (((1,), (1,)), ((), ())), preferred_element_type=jnp.float32
    )
    half = lags // 2
    keep_ref[...] = piece[:half * SUB].reshape(half, 1, SUB, SUB)
    send_ref[...] = piece[half * SUB:].reshape(half, 1, SUB, SUB)


def pieces(index, lags, scaled, halo, partner, start, deps):
    count, subs, hours = index.shape[0], scaled.shape[0], scaled.shape[2]
    half = lags.shape[0] // 2
    out = jax.ShapeDtypeStruct((half, count, SUB, SUB), jnp.float32)

    return pl.pallas_call(
        piece_kernel,
        grid_spec=pltpu.PrefetchScalarGridSpec(
            num_scalar_prefetch=2,
            grid=(count,),
            in_specs=[
                pl.BlockSpec((1, SUB, hours), lambda i, index, lags: (index[i], 0, 0)),
                pl.BlockSpec((1, SUB, LANES), lambda i, index, lags: (index[i], 0, 0)),
                pl.BlockSpec(
                    (1, SUB, LANES), lambda i, index, lags: (subs + lax.div(index[i], PACK), 0, 0)
                ),
                pl.BlockSpec((1, SUB, hours), lambda i, index, lags: (start + i, 0, 0)),
                *[pl.BlockSpec(memory_space=pl.ANY)] * len(deps),
            ],
            out_specs=[pl.BlockSpec((half, 1, SUB, SUB), lambda i, index, lags: (0, i, 0, 0))] * 2,
            scratch_shapes=[
                pltpu.VMEM((SUB, HALO + hours), jnp.bfloat16),
                pltpu.VMEM((2 * half * SUB, hours), jnp.bfloat16),
            ],
        ),
        out_shape=[out, out],
        compiler_params=pltpu.CompilerParams(vmem_limit_bytes=FEW),
        cost_estimate=pl.CostEstimate(flops=1, bytes_accessed=1, transcendentals=0),
        name="pieces",
    )(index, lags, scaled, halo, halo, partner, *deps)


def tile_call(kernel, name, count, inputs, outputs, scalars=(), deps=()):
    def couple(place):
        return pl.BlockSpec((2, 1, SUB, SUB), lambda i: (place, i, 0, 0))

    return pl.pallas_call(
        kernel,
        grid=(count,),
        in_specs=[
            *[couple(place) for _, place in inputs],
            *[pl.BlockSpec(memory_space=pltpu.SMEM)] * len(scalars),
            *[pl.BlockSpec(memory_space=pl.ANY)] * len(deps),
        ],
        out_specs=[couple(0)] * outputs,
        out_shape=[jax.ShapeDtypeStruct((2, count, SUB, SUB), jnp.float32)] * outputs,
        compiler_params=pltpu.CompilerParams(vmem_limit_bytes=FEW),
        cost_estimate=pl.CostEstimate(flops=1, bytes_accessed=1, transcendentals=0),
        name=name,
    )(*[array for array, _ in inputs], *scalars, *deps)


def forward_kernel(keep_ref, one_ref, *refs):
    refs[-1][...] = keep_ref[...] + one_ref[...]


def across_kernel(*refs):
    for order in range(2):
        keep_ref, one_ref, two_ref = refs[3 * order:3 * order + 3]
        total = keep_ref[...] + one_ref[...] + two_ref[...]
        refs[-2][order] = total[0]
        refs[-1][order] = total[1]


def final_kernel(mine_ref, three_ref, divisor_ref, *refs):
    refs[-1][...] = (mine_ref[...] + three_ref[...]) / divisor_ref[0]


def per_device(anomalies, lag_list, pair_plan):
    points, seg_hours = anomalies.shape
    n_grid, n_tm = lax.axis_size("grid"), lax.axis_size("tm")
    all_hours = seg_hours * n_tm
    blocks = anomalies.reshape(points // SUB, SUB, seg_hours)

    def along_tm(value, target):
        return lax.ppermute(value, "tm", [(i, target(i)) for i in range(n_tm)])

    def ring_near(i):
        return i - i % RING + ((i % RING) ^ 1)

    def ring_far(i):
        return i - i % RING + (RING - 1 - i % RING)

    def other_half(i):
        return (i + RING) % n_tm

    def along_grid(value, route):
        return lax.ppermute(value, "grid", [(i, route(i) % n_grid) for i in range(n_grid)])

    routes = (
        lambda i: i + 3 if i % 2 else i + 1,
        lambda i: i + 2,
        lambda i: i + 1 if i % 2 else i + 3,
    )
    back = (
        lambda i: i - 1 if i % 2 else i - 3,
        lambda i: i - 2,
        lambda i: i - 3 if i % 2 else i - 1,
    )
    even = lax.axis_index("grid") % 2 == 0
    plan = pair_plan[0]
    plans = (jnp.where(even, plan[2], plan[0]), plan[1], jnp.where(even, plan[0], plan[2]))
    sums, *seconds = lax.optimization_barrier(
        (local_sums(anomalies, n_tm), *[one[:, 1] for one in plans])
    )
    wanted = jnp.concatenate([along_grid(one, route) for one, route in zip(seconds, back)])
    norm = norms(lax.all_to_all(sums, "tm", 0, 0), all_hours)

    me = lax.axis_index("tm")
    place, part = me % RING, me // RING
    near, far = place ^ 1, RING - 1 - place
    orders = (
        jnp.stack([place, far, near, RING - 1 - near]),
        jnp.stack([place, near, far, far ^ 1]),
    )
    parts = jnp.stack([part, 1 - part]) * RING
    lag_slots = [jnp.take(lag_list, (order[:, None] + parts[None, :]).reshape(-1)) for order in orders]
    divisor = (all_hours - lag_slots[0][0]).astype(jnp.float32)

    scaled, tail, *picked = scaled_parts(wanted, (4, 4), blocks, norm)
    halo = lax.ppermute(tail, "tm", [(i, i + 1) for i in range(n_tm - 1)])
    beside = along_grid(picked[0], routes[0])
    picked += picked_rows(wanted, (8, 4, 4), PAIRS, scaled)
    beside, waiting = lax.optimization_barrier((beside, picked[1]))
    beside = [beside, along_grid(waiting, routes[0])]
    halo, waiting = lax.optimization_barrier((halo, picked[2]))
    over = along_grid(waiting, routes[1])
    divisor = divisor.reshape(1)

    recent = [scaled]

    def step_one(groups, orders=(0, 1)):
        group = []
        for order, (which, first, count, partner, start) in zip(orders, groups):
            index = plans[which][first:first + count, 0]
            keep, send = pieces(index, lag_slots[order], scaled, halo, partner, start, recent)
            recent[:] = [keep]
            group.append((keep, along_tm(send, (ring_near, ring_far)[order])))
        return group

    def step_two(group):
        result = []
        for order, (keep, one) in enumerate(group):
            inputs = [(keep, 1), (one, 1)]
            (forward,) = tile_call(
                forward_kernel, "forward", keep.shape[1], inputs, 1, deps=recent
            )
            recent[:] = [forward]
            result.append((keep, one, along_tm(forward, (ring_far, ring_near)[order])))
        return result

    def step_three(group):
        count = group[0][0].shape[1]
        inputs = [(array, 0) for triple in group for array in triple]
        mine, across = tile_call(across_kernel, "across", count, inputs, 2, deps=recent)
        recent[:] = [mine]
        return mine, along_tm(across, other_half)

    def step_four(mine, three):
        inputs = [(mine, 0), (three, 0)]
        (out,) = tile_call(
            final_kernel, "final", mine.shape[1], inputs, 1, scalars=[divisor], deps=recent
        )
        recent[:] = [out]
        return out.reshape(-1, SUB, SUB)

    a = step_one([(0, 0, 4, beside[0], 0), (0, 4, 4, beside[1], 0)])
    a = step_two(a)
    recent[0], *waiting = lax.optimization_barrier((recent[0], *picked[3:]))
    last = [along_grid(one, routes[2]) for one in waiting]
    b = step_one([(1, 0, 4, over, 0)], (0,))
    a = step_three(a)
    b += step_one([(1, 4, 4, over, 4)], (1,))
    c = step_one([(2, 0, 2, last[0], 0), (2, 2, 2, last[0], 2)])
    b = step_two(b)
    d = step_one([(2, 4, 2, last[1], 0), (2, 6, 2, last[1], 2)])
    c = step_two(c)
    b = step_three(b)
    d = step_two(d)
    c = step_three(c)
    a = step_four(*a)
    b = step_four(*b)
    d = step_three(d)
    c = step_four(*c)
    d = step_four(*d)
    middle = b
    farthest = jnp.concatenate([c, d])
    rows = [jnp.where(even, farthest, a), middle, jnp.where(even, a, farthest)]
    return jnp.stack(rows)[None, :, :, None]


def solution(mesh):
    in_specs = (P("grid", "tm"), P(), P("grid", None, None, None))
    out_specs = P("grid", None, None, "tm", None, None)
    return jax.shard_map(
        per_device, mesh=mesh, in_specs=in_specs, out_specs=out_specs, check_vma=False
    )
```
